128 devices in a mesh: row: 16 (over y_hi, z, core), feat: 8 (over y_lo, x).
Axes of the slice: x: 4, y: 4 (y_hi: 2, y_lo: 2; y = y_hi * 2 + y_lo), z: 4, core: 2. Of those that a mesh axis runs over, the one named last changes fastest.
Arguments:
- queries: float32 [2, 768, 16384], P(None, 'feat', 'row'), may hold values from -6 to 6
- inverse_fisher: float32 [16384, 16384], P('row', 'feat'), as said below
- examples: bfloat16 [24576, 16384], P('row', 'feat'), may hold values from -0.046875 to 0.046875
Outputs:
- scores: float32 [2, 768, 24576], P(None, 'feat', 'row')
The draws below stay inside these ranges and needn't reach their ends.
Inputs may be any that keep to these rules, and one draw needn't show every extreme that they name: `inverse_fisher`: symmetric.
All inputs are finite; a program needn't handle non-finite values.
Results may differ from the reference program's by a relative error of at most 0.0029.
Values may be sent and summed in bfloat16 or wider, within the bound.
A program may use at most 128 MiB of HBM per device.

```python
import math
import jax
import jax.numpy as jnp
from jax import lax

K = 16384
GROUPS = 2
Q = 768
EXAMPLES = 24576


def draw_inverse_fisher(key, part):
    first_key, second_key = jax.random.split(jax.random.fold_in(key, 17))
    random_part = jax.random.normal(first_key, (K, K), jnp.float32)
    diag_values = jnp.exp(jax.random.uniform(second_key, (K,), jnp.float32, math.log(0.5), math.log(2.0)))
    spread = 0.35
    symmetric = (random_part + random_part.T) * (spread / math.sqrt(K))
    identity = jnp.eye(K, dtype=jnp.float32)
    return symmetric + identity * diag_values[:, None]


def shard_levels(key, shape, cuts, least, top_value):
    loudness, own = 1.0, jax.random.fold_in(key, 6)
    for dim, blocks in cuts:
        draws = jnp.exp(jax.random.uniform(jax.random.fold_in(own, dim), (blocks,), jnp.float32, least / len(cuts), top_value / len(cuts)))
        loudness = loudness * jnp.repeat(draws, shape[dim] // blocks).reshape([-1 if axis == dim else 1 for axis in range(len(shape))])
    return loudness


def centred(stream_key, shape, width, reach, cuts=(), kind=jnp.bfloat16):
    gain = shard_levels(stream_key, shape, cuts, -0.22, 0.18) if cuts else 1.0
    entries = jax.random.normal(stream_key, shape, jnp.float32) * width * gain
    return jnp.minimum(jnp.maximum(entries, -reach), reach).astype(kind)


def setup_inputs(seed: int = 0) -> dict:
    keys = jax.random.split(jax.random.key(seed), 4)
    queries = centred(keys[0], (GROUPS, Q, K), 1.0, 6.0, ((1, 8), (2, 16)), jnp.float32)
    inverse_fisher = draw_inverse_fisher(jax.random.fold_in(keys[3], 71), 0)
    examples = centred(keys[2], (EXAMPLES, K), K ** -0.5, 0.046875, ((0, 16), (1, 8)))
    return dict(queries=queries, inverse_fisher=inverse_fisher, examples=examples)


def reference(queries, inverse_fisher, examples):
    results = []
    for group in range(GROUPS):
        precond = jnp.dot(queries[group], inverse_fisher, precision=lax.Precision.HIGHEST, preferred_element_type=jnp.float32).astype(jnp.bfloat16)
        results.append(lax.dot_general(precond, examples, (((1,), (1,)), ((), ())), preferred_element_type=jnp.float32))
    return jnp.stack(results)
```

```python
import functools

import jax
import jax.numpy as jnp
from jax import lax
from jax.experimental import pallas as pl
from jax.experimental.pallas import tpu as pltpu
from jax.sharding import PartitionSpec as P

F32, BF16 = jnp.float32, jnp.bfloat16
SIZES = (32, 32, 32, 32, 32, 16, 16)
CHUNKS = len(SIZES)
PLACES = tuple(divmod(sum(SIZES[:k]), 96) for k in range(CHUNKS))
BIG = 8 * max(SIZES)
POWER = 9
LIFT = 13
SLOTS = 4
PATTERN = (("A", 0), ("D", 3), ("E", 4), ("C", 2), ("G", 6), ("H", 7), ("B", 0), ("R", 1), ("K", 3))


def scale_of(largest):
    scale = jnp.maximum(largest, 2.0**-90).astype(BF16).astype(F32)
    return scale, (2.0**LIFT) / (scale * 0.0625)


def code(value, factor):
    v = (value * 0.0625) * factor
    v2 = v * v
    v4 = v2 * v2
    return (v4 * v4 * v).astype(BF16)


def decode(coded, scale):
    w = coded.astype(F32)
    size = jnp.exp2(jnp.log2(jnp.abs(w)) * (1.0 / POWER) - LIFT) * scale
    return jnp.where(w < 0, -size, jnp.where(w == 0, 0.0, size))


def fold_max(block):
    rows = block.shape[0]
    return jnp.max(jnp.abs(block).reshape(rows // 8, 8, 128), axis=0)


def kernel(q, f_hbm, e_hbm, out, qh, ql, fst, fh, fl, e, pp, cx, qm, psend, pry, pair, prx, pf, ss, srx, ysend, yrx,
           load_sem, e_sem, q_s, q_r, cx_s, cx_r, h_s, h_r, p_s, p_r, g_s, g_r, k_s, k_r, s_s, s_r, y_s, y_r):
    r, f = lax.axis_index("row"), lax.axis_index("feat")
    x, yl = f % 4, f // 4
    c, chip = r % 2, r // 2
    z, yh = chip % 4, chip // 4
    sibling = (chip * 2 + (1 - c), f)
    ypeer = (r, (1 - yl) * 4 + x)

    def xpeer(d):
        return (r, yl * 4 + (x + d) % 4)

    def chip_at(j):
        return ((yh + j // 4) % 2) * 4 + (z + j % 4) % 4

    def rpeer(j):
        return (chip_at(j) * 2 + c, f)

    def remote(src, dst, send, recv, device):
        return pltpu.make_async_remote_copy(
            src_ref=src, dst_ref=dst, send_sem=send, recv_sem=recv, device_id=device,
            device_id_type=pl.DeviceIdType.MESH)

    def load_f(i, slot):
        return pltpu.make_async_copy(f_hbm.at[pl.ds(i * 128, 128), :], fst.at[slot], load_sem.at[slot])

    for i in range(SLOTS):
        load_f(i, i).start()
    load_e = pltpu.make_async_copy(e_hbm, e, e_sem.at[0])

    peers = [sibling, ypeer] + [xpeer(d) for d in (1, 2, 3)] + [rpeer(j) for j in range(1, 8)]
    barrier = pltpu.get_barrier_semaphore()
    for peer in peers:
        pl.semaphore_signal(barrier, inc=1, device_id=peer, device_id_type=pl.DeviceIdType.MESH)

    def code_queries(k):
        (group, first), own, m = PLACES[k], SIZES[k], 8 * SIZES[k]
        largest = jnp.zeros((8, 128), F32)
        for b in range(8):
            largest = jnp.maximum(largest, fold_max(q[group, first:first + own, b * 128:(b + 1) * 128]))
        scale, factor = scale_of(jnp.max(largest, axis=0, keepdims=True))
        for b in range(8):
            qm[k][0, b * own:(b + 1) * own, :] = code(q[group, first:first + own, b * 128:(b + 1) * 128], factor)
        qm[k][0, m:m + 16, :] = jnp.broadcast_to(scale, (16, 128)).astype(BF16)

    def q_y(k):
        return remote(qm[k].at[0], qm[k].at[4], q_s.at[k, 4], q_r.at[k, 4], ypeer)

    def q_x(k, s, d):
        return remote(qm[k].at[s], qm[k].at[s + d], q_s.at[k, s + d], q_r.at[k, s + d], xpeer(d))

    code_queries(0)
    pl.semaphore_wait(barrier, len(peers))
    for k in range(CHUNKS):
        if k:
            code_queries(k)
        q_y(k).start()
        if k == 0:
            for d in (2, 1, 3):
                q_x(0, 0, d).start()

    def split_f(i):
        slot = i % SLOTS
        load_f(i, slot).wait()
        for half in range(2):
            part = fst[slot, :, half * 1024:(half + 1) * 1024]
            high = part.astype(BF16)
            rows = pl.ds(pl.multiple_of(i * 128, 128), 128)
            fh[half, rows, :] = high
            fl[half, rows, :] = (part - high.astype(F32)).astype(BF16)

        @pl.when(i + SLOTS < 8)
        def _():
            load_f(i + SLOTS, slot).start()

    def forward(k):
        q_y(k).wait_recv()
        for d in (2, 1, 3):
            q_x(k, 4, d).start()
        if k + 1 < CHUNKS:
            for d in (2, 1, 3):
                q_x(k + 1, 0, d).start()

    forward(0)
    forward(1)
    lax.fori_loop(0, 4, lambda i, _: (split_f(i), 0)[1], 0)
    forward(2)
    lax.fori_loop(4, 8, lambda i, _: (split_f(i), 0)[1], 0)
    forward(3)
    load_e.start()

    def cross(k):
        return remote(pp.at[1 - c, 0:8 * SIZES[k]], cx.at[k % 2, 0:8 * SIZES[k]], cx_s.at[k], cx_r.at[k], sibling)

    def stage_a(k):
        own, m = SIZES[k], 8 * SIZES[k]
        if k + 4 < CHUNKS:
            forward(k + 4)
        for j in range(8):
            if j % 4:
                q_x(k, j // 4 * 4, j % 4).wait_recv()
            place = (((x + 4 - j % 4) % 4) * 2 + (yl + j // 4) % 2) * own
            rows = pl.ds(pl.multiple_of(place, 16), own)
            scale = qm[k][j, m:m + 16, :].astype(F32)[0:1]
            for b in range(8):
                value = decode(qm[k][j, b * own:(b + 1) * own, :], scale)
                high = value.astype(BF16)
                qh[rows, b * 128:(b + 1) * 128] = high
                ql[rows, b * 128:(b + 1) * 128] = (value - high.astype(F32)).astype(BF16)
        if k:
            cross(k - 1).wait_send()

        def product(half):
            @pl.loop(0, 2)
            def _(n):
                cols = pl.ds(pl.multiple_of(n * 512, 512), 512)
                total = jnp.dot(qh[0:m, :], fh[half, :, cols], preferred_element_type=F32)
                total += jnp.dot(qh[0:m, :], fl[half, :, cols], preferred_element_type=F32)
                total += jnp.dot(ql[0:m, :], fh[half, :, cols], preferred_element_type=F32)
                pp[half, 0:m, cols] = total

        product(1 - c)
        cross(k).start()
        product(c)

    def h_to(k):
        return remote(psend[k].at[pl.ds((1 - yh) * 4, 4)], pry[k], h_s.at[k], h_r.at[k], rpeer(4))

    def p_to(k, d):
        return remote(pair[k].at[(z + d) % 4], prx[k].at[d - 1], p_s.at[k, d], p_r.at[k, d], rpeer(d))

    def put_coded(m, tiles, ref, b):
        step = m // len(tiles)
        largest = functools.reduce(jnp.maximum, [fold_max(tile) for tile in tiles])
        scale, factor = scale_of(jnp.max(largest, axis=0, keepdims=True))
        for t, tile in enumerate(tiles):
            ref[b, t * step:(t + 1) * step, :] = code(tile, factor)
        ref[b, m:m + 16, :] = jnp.broadcast_to(scale, (16, 128)).astype(BF16)

    def stage_b(k):
        m = 8 * SIZES[k]
        step = m // 4
        cross(k).wait_recv()

        @pl.loop(0, 8)
        def _(b):
            cols = pl.ds(pl.multiple_of(b * 128, 128), 128)
            put_coded(m, [pp[c, t:t + step, cols] + cx[k % 2, t:t + step, cols] for t in range(0, m, step)], psend[k], b)

        h_to(k).start()

    def stage_r(k):
        m = 8 * SIZES[k]
        step = m // 4
        h_to(k).wait_recv()

        @pl.loop(0, 4)
        def _(b):
            mine_scale = psend[k][yh * 4 + b, m:m + 16, :].astype(F32)[0:1]
            scale = pry[k][b, m:m + 16, :].astype(F32)[0:1]
            put_coded(m, [decode(psend[k][yh * 4 + b, t:t + step, :], mine_scale) + decode(pry[k][b, t:t + step, :], scale)
                          for t in range(0, m, step)], pair[k], b)

        for d in (2, 1, 3):
            p_to(k, d).start()

    mine = c * 8 + chip

    def g_y(k):
        return remote(pf[k].at[mine], pf[k].at[mine], g_s.at[k, 4], g_r.at[k, 4], rpeer(4))

    def g_z(k, s, d):
        piece = c * 8 + chip_at(s)
        return remote(pf[k].at[piece], pf[k].at[piece], g_s.at[k, s + d], g_r.at[k, s + d], rpeer(d))

    def stage_c(k):
        m, step = 8 * SIZES[k], SIZES[k]
        for d in (1, 2, 3):
            p_to(k, d).wait_recv()
        scales = [pair[k][z, m:m + 16, :].astype(F32)[0:1]]
        scales += [prx[k][d, m:m + 16, :].astype(F32)[0:1] for d in range(3)]

        @pl.loop(0, 8)
        def _(t):
            rows = pl.ds(pl.multiple_of(t * step, 16), step)
            total = decode(pair[k][z, rows, :], scales[0])
            for d in range(3):
                total += decode(prx[k][d, rows, :], scales[d + 1])
            pf[k][mine, rows, :] = total.astype(BF16)

        g_y(k).start()
        for d in (1, 3, 2):
            g_z(k, 0, d).start()

    def stage_d(k):
        g_y(k).wait_recv()
        for d in (1, 3, 2):
            g_z(k, 4, d).start()

    def whole(k):
        return remote(pf[k].at[pl.ds(c * 8, 8)], pf[k].at[pl.ds(c * 8, 8)], k_s.at[k], k_r.at[k], sibling)

    def stage_k(k):
        for s in (0, 4):
            for d in (1, 3, 2):
                g_z(k, s, d).wait_recv()
        whole(k).start()

    def s_to(k, d):
        return remote(ss[k].at[(x + d) % 4], srx[k].at[d - 1], s_s.at[k, d - 1], s_r.at[k, d - 1], xpeer(d))

    def stage_e(k):
        if k == 0:
            load_e.wait()
        whole(k).wait_recv()

        @pl.loop(0, 3)
        def _(n):
            rows = pl.ds(pl.multiple_of(n * 512, 512), 512)
            left = jnp.concatenate([pf[k][g] for g in range(16)], axis=1)
            total = lax.dot_general(left, e[rows, :], (((1,), (1,)), ((), ())), preferred_element_type=F32)
            ss[k][:, :, rows] = total.astype(BF16).reshape(4, 2 * SIZES[k], 512)

        for d in (1, 3, 2):
            s_to(k, d).start()

    def y_to(k):
        return remote(ysend[k], yrx[k], y_s.at[k], y_r.at[k], ypeer)

    def stage_g(k):
        (group, first), own = PLACES[k], SIZES[k]
        for d in (1, 2, 3):
            s_to(k, d).wait_recv()

        def summed(part, rows, cols):
            rows = pl.ds(pl.multiple_of(part * own + rows, 16), 16)
            total = ss[k][x, rows, cols].astype(F32)
            for d in range(3):
                total += srx[k][d, rows, cols].astype(F32)
            return total

        @pl.loop(0, 3)
        def _(n):
            cols = pl.ds(pl.multiple_of(n * 512, 512), 512)
            for t in range(0, own, 16):
                ysend[k][t:t + 16, cols] = summed(1 - yl, t, cols).astype(BF16)

        y_to(k).start()

        @pl.loop(0, 3)
        def _(n):
            cols = pl.ds(pl.multiple_of(n * 512, 512), 512)
            for t in range(0, own, 16):
                out[group, first + t:first + t + 16, cols] = summed(yl, t, cols)

    def stage_h(k):
        (group, first), own = PLACES[k], SIZES[k]
        y_to(k).wait_recv()

        @pl.loop(0, 3)
        def _(n):
            cols = pl.ds(pl.multiple_of(n * 512, 512), 512)
            out[group, first:first + own, cols] += yrx[k][:, cols].astype(F32)

    stages = dict(A=stage_a, B=stage_b, R=stage_r, C=stage_c, D=stage_d, K=stage_k, E=stage_e, G=stage_g, H=stage_h)
    for turn in range(CHUNKS + max(late for _, late in PATTERN)):
        for name, late in PATTERN:
            if 0 <= turn - late < CHUNKS:
                stages[name](turn - late)

    for k in range(CHUNKS):
        q_y(k).wait_send()
        for s in (0, 4):
            for d in (1, 2, 3):
                q_x(k, s, d).wait_send()
                g_z(k, s, d).wait_send()
        h_to(k).wait_send()
        for d in (1, 2, 3):
            p_to(k, d).wait_send()
        g_y(k).wait_send()
        whole(k).wait_send()
        for d in (1, 2, 3):
            s_to(k, d).wait_send()
        y_to(k).wait_send()
    cross(CHUNKS - 1).wait_send()


def body(queries, inverse_fisher, examples):
    dma = pltpu.SemaphoreType.DMA
    n = CHUNKS

    def each(shape):
        return [pltpu.VMEM(shape(o), BF16) for o in SIZES]

    return pl.pallas_call(
        kernel,
        out_shape=jax.ShapeDtypeStruct((2, 96, 1536), F32),
        in_specs=[pl.BlockSpec(memory_space=pltpu.VMEM), pl.BlockSpec(memory_space=pl.ANY),
                  pl.BlockSpec(memory_space=pl.ANY)],
        out_specs=pl.BlockSpec(memory_space=pltpu.VMEM),
        scratch_shapes=[
            pltpu.VMEM((BIG, 1024), BF16),
            pltpu.VMEM((BIG, 1024), BF16),
            pltpu.VMEM((SLOTS, 128, 2048), F32),
            pltpu.VMEM((2, 1024, 1024), BF16),
            pltpu.VMEM((2, 1024, 1024), BF16),
            pltpu.VMEM((1536, 2048), BF16),
            pltpu.VMEM((2, BIG, 1024), F32),
            pltpu.VMEM((2, BIG, 1024), F32),
            each(lambda o: (8, 8 * o + 16, 128)),
            each(lambda o: (8, 8 * o + 16, 128)),
            each(lambda o: (4, 8 * o + 16, 128)),
            each(lambda o: (4, 8 * o + 16, 128)),
            each(lambda o: (3, 8 * o + 16, 128)),
            each(lambda o: (16, 8 * o, 128)),
            each(lambda o: (4, 2 * o, 1536)),
            each(lambda o: (3, 2 * o, 1536)),
            each(lambda o: (o, 1536)),
            each(lambda o: (o, 1536)),
            dma((SLOTS,)), dma((1,)),
            dma((n, 8)), dma((n, 8)),
            dma((n,)), dma((n,)),
            dma((n,)), dma((n,)),
            dma((n, 4)), dma((n, 4)),
            dma((n, 8)), dma((n, 8)),
            dma((n,)), dma((n,)),
            dma((n, 3)), dma((n, 3)),
            dma((n,)), dma((n,)),
        ],
        compiler_params=pltpu.CompilerParams(
            collective_id=0, has_side_effects=True, vmem_limit_bytes=60 * 2**20),
        cost_estimate=pl.CostEstimate(flops=29_000_000_000, bytes_accessed=17_000_000, transcendentals=0),
        name="influence",
    )(queries, inverse_fisher, examples)


def solution(mesh):
    return jax.shard_map(
        body,
        mesh=mesh,
        in_specs=(P(None, "feat", "row"), P("row", "feat"), P("row", "feat")),
        out_specs=P(None, "feat", "row"),
        check_vma=False,
    )
```

```python
import functools
import math

import jax
import jax.numpy as jnp
from jax import lax
from jax.experimental import pallas as pl
from jax.experimental.pallas import tpu as pltpu
from jax.sharding import PartitionSpec as P

F32, BF16 = jnp.float32, jnp.bfloat16
SIZES = (32, 32, 32, 32, 32, 16, 16)
CHUNKS = len(SIZES)
PLACES = tuple(divmod(sum(SIZES[:k]), 96) for k in range(CHUNKS))
BIG = 8 * max(SIZES)
POWER = 9
LIFT = 13
ROOT = 1.0 / (POWER * math.log(2.0))
SLOTS = 4
ACROSS = (5,)
PATTERN = (("A", 0), ("D", 3), ("E", 4), ("C", 2), ("G", 6), ("H", 7), ("B", 0), ("R", 1), ("K", 3))


def scale_of(largest):
    scale = jnp.maximum(largest, 2.0**-90).astype(BF16).astype(F32)
    return scale, (2.0**LIFT) / (scale * 0.0625)


def code(value, factor):
    v = (value * 0.0625) * factor
    v2 = v * v
    v4 = v2 * v2
    return (v4 * v4 * v).astype(BF16)


def decode(coded, scale):
    w = coded.astype(F32)
    size = jnp.exp2(jnp.log(jnp.abs(w)) * ROOT) * (scale * 2.0**-LIFT)
    return jnp.where(w < 0, -size, size)


def fold_max(block):
    rows = block.shape[0]
    return jnp.max(jnp.abs(block).reshape(rows // 8, 8, 128), axis=0)


def kernel(q, f_hbm, e_hbm, out, qh, ql, fst, fh, fl, e, pp, cx, qm, psend, pry, pair, prx, pf, ss, srx, ysend, yrx,
           load_sem, e_sem, q_s, q_r, cx_s, cx_r, h_s, h_r, p_s, p_r, g_s, g_r, k_s, k_r, s_s, s_r, y_s, y_r):
    r, f = lax.axis_index("row"), lax.axis_index("feat")
    x, yl = f % 4, f // 4
    c, chip = r % 2, r // 2
    z, yh = chip % 4, chip // 4
    sibling = (chip * 2 + (1 - c), f)
    ypeer = (r, (1 - yl) * 4 + x)

    def xpeer(d):
        return (r, yl * 4 + (x + d) % 4)

    def chip_at(j):
        return ((yh + j // 4) % 2) * 4 + (z + j % 4) % 4

    def rpeer(j):
        return (chip_at(j) * 2 + c, f)

    def remote(src, dst, send, recv, device):
        return pltpu.make_async_remote_copy(
            src_ref=src, dst_ref=dst, send_sem=send, recv_sem=recv, device_id=device,
            device_id_type=pl.DeviceIdType.MESH)

    def load_f(i, slot):
        return pltpu.make_async_copy(f_hbm.at[pl.ds(i * 128, 128), :], fst.at[slot], load_sem.at[slot])

    for i in range(SLOTS):
        load_f(i, i).start()
    load_e = pltpu.make_async_copy(e_hbm, e, e_sem.at[0])

    peers = [sibling, ypeer] + [xpeer(d) for d in (1, 2, 3)] + [rpeer(j) for j in range(1, 8)]
    barrier = pltpu.get_barrier_semaphore()
    for peer in peers:
        pl.semaphore_signal(barrier, inc=1, device_id=peer, device_id_type=pl.DeviceIdType.MESH)

    def code_queries(k):
        (group, first), own, m = PLACES[k], SIZES[k], 8 * SIZES[k]
        largest = jnp.zeros((8, 128), F32)
        for b in range(8):
            largest = jnp.maximum(largest, fold_max(q[group, first:first + own, b * 128:(b + 1) * 128]))
        scale, factor = scale_of(jnp.max(largest, axis=0, keepdims=True))
        for b in range(8):
            qm[k][0, b * own:(b + 1) * own, :] = code(q[group, first:first + own, b * 128:(b + 1) * 128], factor)
        qm[k][0, m:m + 16, :] = jnp.broadcast_to(scale, (16, 128)).astype(BF16)

    def q_y(k):
        return remote(qm[k].at[0], qm[k].at[4], q_s.at[k, 4], q_r.at[k, 4], ypeer)

    def q_x(k, s, d):
        return remote(qm[k].at[s], qm[k].at[s + d], q_s.at[k, s + d], q_r.at[k, s + d], xpeer(d))

    code_queries(0)
    pl.semaphore_wait(barrier, len(peers))
    for k in range(CHUNKS):
        if k:
            code_queries(k)
        q_y(k).start()
        if k == 0:
            for d in (2, 1, 3):
                q_x(0, 0, d).start()

    def split_f(i):
        slot = i % SLOTS
        load_f(i, slot).wait()
        for half in range(2):
            part = fst[slot, :, half * 1024:(half + 1) * 1024]
            high = part.astype(BF16)
            rows = pl.ds(pl.multiple_of(i * 128, 128), 128)
            fh[half, rows, :] = high
            fl[half, rows, :] = (part - high.astype(F32)).astype(BF16)

        @pl.when(i + SLOTS < 8)
        def _():
            load_f(i + SLOTS, slot).start()

    def forward(k):
        q_y(k).wait_recv()
        for d in (2, 1, 3):
            q_x(k, 4, d).start()
        if k + 1 < CHUNKS:
            for d in (2, 1, 3):
                q_x(k + 1, 0, d).start()

    forward(0)
    forward(1)
    lax.fori_loop(0, 4, lambda i, _: (split_f(i), 0)[1], 0)
    forward(2)
    lax.fori_loop(4, 8, lambda i, _: (split_f(i), 0)[1], 0)
    forward(3)
    load_e.start()

    def cross(k):
        return remote(pp.at[1 - c, 0:8 * SIZES[k]], cx.at[k % 2, 0:8 * SIZES[k]], cx_s.at[k], cx_r.at[k], sibling)

    def stage_a(k):
        own, m = SIZES[k], 8 * SIZES[k]
        if k + 4 < CHUNKS:
            forward(k + 4)
        for j in range(8):
            if j % 4:
                q_x(k, j // 4 * 4, j % 4).wait_recv()
            place = (((x + 4 - j % 4) % 4) * 2 + (yl + j // 4) % 2) * own
            rows = pl.ds(pl.multiple_of(place, 16), own)
            scale = qm[k][j, m:m + 16, :].astype(F32)[0:1]
            for b in range(8):
                value = decode(qm[k][j, b * own:(b + 1) * own, :], scale)
                high = value.astype(BF16)
                qh[rows, b * 128:(b + 1) * 128] = high
                ql[rows, b * 128:(b + 1) * 128] = (value - high.astype(F32)).astype(BF16)
        if k:
            cross(k - 1).wait_send()

        def product(half):
            @pl.loop(0, 2)
            def _(n):
                cols = pl.ds(pl.multiple_of(n * 512, 512), 512)
                total = jnp.dot(qh[0:m, :], fh[half, :, cols], preferred_element_type=F32)
                total += jnp.dot(qh[0:m, :], fl[half, :, cols], preferred_element_type=F32)
                total += jnp.dot(ql[0:m, :], fh[half, :, cols], preferred_element_type=F32)
                pp[half, 0:m, cols] = total

        product(1 - c)
        cross(k).start()
        product(c)

    def h_to(k):
        return remote(psend[k].at[pl.ds((1 - yh) * 4, 4)], pry[k], h_s.at[k], h_r.at[k], rpeer(4))

    def p_to(k, d):
        return remote(pair[k].at[(z + d) % 4], prx[k].at[d - 1], p_s.at[k, d], p_r.at[k, d], rpeer(d))

    def put_coded(m, tiles, ref, b):
        step = m // len(tiles)
        largest = functools.reduce(jnp.maximum, [fold_max(tile) for tile in tiles])
        scale, factor = scale_of(jnp.max(largest, axis=0, keepdims=True))
        for t, tile in enumerate(tiles):
            ref[b, t * step:(t + 1) * step, :] = code(tile, factor)
        ref[b, m:m + 16, :] = jnp.broadcast_to(scale, (16, 128)).astype(BF16)

    def stage_b(k):
        m = 8 * SIZES[k]
        step = m // 4
        cross(k).wait_recv()

        @pl.loop(0, 8)
        def _(b):
            cols = pl.ds(pl.multiple_of(b * 128, 128), 128)
            put_coded(m, [pp[c, t:t + step, cols] + cx[k % 2, t:t + step, cols] for t in range(0, m, step)], psend[k], b)

        h_to(k).start()

    def stage_r(k):
        m = 8 * SIZES[k]
        step = m // 4
        h_to(k).wait_recv()

        @pl.loop(0, 4)
        def _(b):
            mine_scale = psend[k][yh * 4 + b, m:m + 16, :].astype(F32)[0:1]
            scale = pry[k][b, m:m + 16, :].astype(F32)[0:1]
            put_coded(m, [decode(psend[k][yh * 4 + b, t:t + step, :], mine_scale) + decode(pry[k][b, t:t + step, :], scale)
                          for t in range(0, m, step)], pair[k], b)

        for d in (2, 1, 3):
            p_to(k, d).start()

    mine = c * 8 + chip

    def g_y(k):
        return remote(pf[k].at[mine], pf[k].at[mine], g_s.at[k, 4], g_r.at[k, 4], rpeer(4))

    def g_z(k, s, d):
        piece = c * 8 + chip_at(s)
        return remote(pf[k].at[piece], pf[k].at[piece], g_s.at[k, s + d], g_r.at[k, s + d], rpeer(d))

    def stage_c(k):
        m, step = 8 * SIZES[k], SIZES[k]
        for d in (1, 2, 3):
            p_to(k, d).wait_recv()
        scales = [pair[k][z, m:m + 16, :].astype(F32)[0:1]]
        scales += [prx[k][d, m:m + 16, :].astype(F32)[0:1] for d in range(3)]

        @pl.loop(0, 8)
        def _(t):
            rows = pl.ds(pl.multiple_of(t * step, 16), step)
            total = decode(pair[k][z, rows, :], scales[0])
            for d in range(3):
                total += decode(prx[k][d, rows, :], scales[d + 1])
            pf[k][mine, rows, :] = total.astype(BF16)

        g_y(k).start()
        for d in (1, 3, 2):
            g_z(k, 0, d).start()

    def stage_d(k):
        g_y(k).wait_recv()
        for d in (1, 3, 2):
            g_z(k, 4, d).start()

    def whole(k):
        return remote(pf[k].at[pl.ds(c * 8, 8)], pf[k].at[pl.ds(c * 8, 8)], k_s.at[k], k_r.at[k], sibling)

    def stage_k(k):
        for s in (0, 4):
            for d in (1, 3, 2):
                g_z(k, s, d).wait_recv()
        whole(k).start()

    def s_to(k, d):
        if k in ACROSS:
            src, dst = ysend[k].at[(x + d) % 4], srx[k].at[d - 1, 0:SIZES[k]]
        else:
            src, dst = ss[k].at[(x + d) % 4], srx[k].at[d - 1]
        return remote(src, dst, s_s.at[k, d - 1], s_r.at[k, d - 1], xpeer(d))

    def y_to(k):
        own = SIZES[k]
        if k in ACROSS:
            src = ss[k].at[:, pl.ds(pl.multiple_of((1 - yl) * own, 16), own), :]
        else:
            src = ysend[k]
        return remote(src, yrx[k], y_s.at[k], y_r.at[k], ypeer)

    def stage_e(k):
        if k == 0:
            load_e.wait()
        whole(k).wait_recv()

        @pl.loop(0, 3)
        def _(n):
            rows = pl.ds(pl.multiple_of(n * 512, 512), 512)
            left = jnp.concatenate([pf[k][g] for g in range(16)], axis=1)
            total = lax.dot_general(left, e[rows, :], (((1,), (1,)), ((), ())), preferred_element_type=F32)
            ss[k][:, :, rows] = total.astype(BF16).reshape(4, 2 * SIZES[k], 512)

        if k in ACROSS:
            y_to(k).start()
        else:
            for d in (1, 3, 2):
                s_to(k, d).start()

    def across(k):
        (group, first), own = PLACES[k], SIZES[k]
        y_to(k).wait_recv()

        def summed(b, t, cols):
            rows = pl.ds(pl.multiple_of(yl * own + t, 16), 16)
            return ss[k][b, rows, cols].astype(F32) + yrx[k][b, t:t + 16, cols].astype(F32)

        @pl.loop(0, 3)
        def _(n):
            cols = pl.ds(pl.multiple_of(n * 512, 512), 512)
            for t in range(0, own, 16):
                for b in range(4):
                    ysend[k][b, t:t + 16, cols] = summed(b, t, cols).astype(BF16)

        for d in (1, 3, 2):
            s_to(k, d).start()

        @pl.loop(0, 3)
        def _(n):
            cols = pl.ds(pl.multiple_of(n * 512, 512), 512)
            for t in range(0, own, 16):
                out[group, first + t:first + t + 16, cols] = summed(x, t, cols)

    def stage_g(k):
        if k in ACROSS:
            across(k)
            return
        (group, first), own = PLACES[k], SIZES[k]
        for d in (1, 2, 3):
            s_to(k, d).wait_recv()

        def summed(part, rows, cols):
            rows = pl.ds(pl.multiple_of(part * own + rows, 16), 16)
            total = ss[k][x, rows, cols].astype(F32)
            for d in range(3):
                total += srx[k][d, rows, cols].astype(F32)
            return total

        @pl.loop(0, 3)
        def _(n):
            cols = pl.ds(pl.multiple_of(n * 512, 512), 512)
            for t in range(0, own, 16):
                ysend[k][t:t + 16, cols] = summed(1 - yl, t, cols).astype(BF16)

        y_to(k).start()

        @pl.loop(0, 3)
        def _(n):
            cols = pl.ds(pl.multiple_of(n * 512, 512), 512)
            for t in range(0, own, 16):
                out[group, first + t:first + t + 16, cols] = summed(yl, t, cols)

    def stage_h(k):
        (group, first), own = PLACES[k], SIZES[k]
        if k in ACROSS:
            for d in (1, 2, 3):
                s_to(k, d).wait_recv()
        else:
            y_to(k).wait_recv()

        @pl.loop(0, 3)
        def _(n):
            cols = pl.ds(pl.multiple_of(n * 512, 512), 512)
            if k in ACROSS:
                for t in range(0, own, 16):
                    rows = slice(first + t, first + t + 16)
                    out[group, rows, cols] += sum(srx[k][d, t:t + 16, cols].astype(F32) for d in range(3))
                return
            out[group, first:first + own, cols] += yrx[k][:, cols].astype(F32)

    stages = dict(A=stage_a, B=stage_b, R=stage_r, C=stage_c, D=stage_d, K=stage_k, E=stage_e, G=stage_g, H=stage_h)
    for turn in range(CHUNKS + max(late for _, late in PATTERN)):
        for name, late in PATTERN:
            if 0 <= turn - late < CHUNKS:
                stages[name](turn - late)

    for k in range(CHUNKS):
        q_y(k).wait_send()
        for s in (0, 4):
            for d in (1, 2, 3):
                q_x(k, s, d).wait_send()
                g_z(k, s, d).wait_send()
        h_to(k).wait_send()
        for d in (1, 2, 3):
            p_to(k, d).wait_send()
        g_y(k).wait_send()
        whole(k).wait_send()
        for d in (1, 2, 3):
            s_to(k, d).wait_send()
        y_to(k).wait_send()
    cross(CHUNKS - 1).wait_send()


def body(queries, inverse_fisher, examples):
    dma = pltpu.SemaphoreType.DMA
    n = CHUNKS

    def each(shape):
        return [pltpu.VMEM(shape(o), BF16) for o in SIZES]

    return pl.pallas_call(
        kernel,
        out_shape=jax.ShapeDtypeStruct((2, 96, 1536), F32),
        in_specs=[pl.BlockSpec(memory_space=pltpu.VMEM), pl.BlockSpec(memory_space=pl.ANY),
                  pl.BlockSpec(memory_space=pl.ANY)],
        out_specs=pl.BlockSpec(memory_space=pltpu.VMEM),
        scratch_shapes=[
            pltpu.VMEM((BIG, 1024), BF16),
            pltpu.VMEM((BIG, 1024), BF16),
            pltpu.VMEM((SLOTS, 128, 2048), F32),
            pltpu.VMEM((2, 1024, 1024), BF16),
            pltpu.VMEM((2, 1024, 1024), BF16),
            pltpu.VMEM((1536, 2048), BF16),
            pltpu.VMEM((2, BIG, 1024), F32),
            pltpu.VMEM((2, BIG, 1024), F32),
            each(lambda o: (8, 8 * o + 16, 128)),
            each(lambda o: (8, 8 * o + 16, 128)),
            each(lambda o: (4, 8 * o + 16, 128)),
            each(lambda o: (4, 8 * o + 16, 128)),
            each(lambda o: (3, 8 * o + 16, 128)),
            each(lambda o: (16, 8 * o, 128)),
            each(lambda o: (4, 2 * o, 1536)),
            each(lambda o: (3, 2 * o, 1536)),
            [pltpu.VMEM((4, o, 1536) if k in ACROSS else (o, 1536), BF16) for k, o in enumerate(SIZES)],
            [pltpu.VMEM((4, o, 1536) if k in ACROSS else (o, 1536), BF16) for k, o in enumerate(SIZES)],
            dma((SLOTS,)), dma((1,)),
            dma((n, 8)), dma((n, 8)),
            dma((n,)), dma((n,)),
            dma((n,)), dma((n,)),
            dma((n, 4)), dma((n, 4)),
            dma((n, 8)), dma((n, 8)),
            dma((n,)), dma((n,)),
            dma((n, 3)), dma((n, 3)),
            dma((n,)), dma((n,)),
        ],
        compiler_params=pltpu.CompilerParams(
            collective_id=0, has_side_effects=True, vmem_limit_bytes=60 * 2**20),
        cost_estimate=pl.CostEstimate(flops=29_000_000_000, bytes_accessed=17_000_000, transcendentals=0),
        name="influence",
    )(queries, inverse_fisher, examples)


def solution(mesh):
    return jax.shard_map(
        body,
        mesh=mesh,
        in_specs=(P(None, "feat", "row"), P("row", "feat"), P("row", "feat")),
        out_specs=P(None, "feat", "row"),
        check_vma=False,
    )
```

```python
import functools
import math

import jax
import jax.numpy as jnp
from jax import lax
from jax.experimental import pallas as pl
from jax.experimental.pallas import tpu as pltpu
from jax.sharding import PartitionSpec as P

F32, BF16 = jnp.float32, jnp.bfloat16
SIZES = (32, 32, 32, 32, 32, 16, 16)
CHUNKS = len(SIZES)
PLACES = tuple(divmod(sum(SIZES[:k]), 96) for k in range(CHUNKS))
BIG = 8 * max(SIZES)
POWER = 9
LIFT = 13
ROOT = 1.0 / (POWER * math.log(2.0))
SLOTS = 4
ACROSS = (5,)
PATTERN = (("A", 0), ("D", 3), ("E", 4), ("C", 2), ("G", 6), ("H", 7), ("B", 0), ("R", 1), ("K", 3))


def scale_of(largest):
    scale = jnp.maximum(largest, 2.0**-90).astype(BF16).astype(F32)
    return scale, (2.0**LIFT) / (scale * 0.0625)


def code(value, factor):
    v = (value * 0.0625) * factor
    v2 = v * v
    v4 = v2 * v2
    return (v4 * v4 * v).astype(BF16)


def decode(coded, scale):
    w = coded.astype(F32)
    size = jnp.exp2(jnp.log(jnp.abs(w)) * ROOT) * (scale * 2.0**-LIFT)
    return jnp.where(w < 0, -size, size)


def fold_max(block):
    rows = block.shape[0]
    return jnp.max(jnp.abs(block).reshape(rows // 8, 8, 128), axis=0)


def kernel(q, f_hbm, e_hbm, out, qh, ql, fst, fh, fl, e, pp, cx, qm, psend, pry, pair, prx, pf, ss, srx, ysend, yrx,
           load_sem, e_sem, q_s, q_r, cx_s, cx_r, h_s, h_r, p_s, p_r, g_s, g_r, k_s, k_r, s_s, s_r, y_s, y_r):
    r, f = lax.axis_index("row"), lax.axis_index("feat")
    x, yl = f % 4, f // 4
    c, chip = r % 2, r // 2
    z, yh = chip % 4, chip // 4
    sibling = (chip * 2 + (1 - c), f)
    ypeer = (r, (1 - yl) * 4 + x)

    def xpeer(d):
        return (r, yl * 4 + (x + d) % 4)

    def chip_at(j):
        return ((yh + j // 4) % 2) * 4 + (z + j % 4) % 4

    def rpeer(j):
        return (chip_at(j) * 2 + c, f)

    def remote(src, dst, send, recv, device):
        return pltpu.make_async_remote_copy(
            src_ref=src, dst_ref=dst, send_sem=send, recv_sem=recv, device_id=device,
            device_id_type=pl.DeviceIdType.MESH)

    def load_f(i, slot):
        return pltpu.make_async_copy(f_hbm.at[pl.ds(i * 128, 128), :], fst.at[slot], load_sem.at[slot])

    for i in range(SLOTS):
        load_f(i, i).start()
    load_e = pltpu.make_async_copy(e_hbm, e, e_sem.at[0])

    peers = [sibling, ypeer] + [xpeer(d) for d in (1, 2, 3)] + [rpeer(j) for j in range(1, 8)]
    barrier = pltpu.get_barrier_semaphore()
    for peer in peers:
        pl.semaphore_signal(barrier, inc=1, device_id=peer, device_id_type=pl.DeviceIdType.MESH)

    def code_queries(k):
        (group, first), own, m = PLACES[k], SIZES[k], 8 * SIZES[k]
        largest = jnp.zeros((8, 128), F32)
        for b in range(8):
            largest = jnp.maximum(largest, fold_max(q[group, first:first + own, b * 128:(b + 1) * 128]))
        scale, factor = scale_of(jnp.max(largest, axis=0, keepdims=True))
        for b in range(8):
            qm[k][0, b * own:(b + 1) * own, :] = code(q[group, first:first + own, b * 128:(b + 1) * 128], factor)
        qm[k][0, m:m + 16, :] = jnp.broadcast_to(scale, (16, 128)).astype(BF16)

    def q_y(k):
        return remote(qm[k].at[0], qm[k].at[4], q_s.at[k, 4], q_r.at[k, 4], ypeer)

    def q_x(k, s, d):
        return remote(qm[k].at[s], qm[k].at[s + d], q_s.at[k, s + d], q_r.at[k, s + d], xpeer(d))

    code_queries(0)
    pl.semaphore_wait(barrier, len(peers))
    for k in range(CHUNKS):
        if k:
            code_queries(k)
        q_y(k).start()
        if k == 0:
            for d in (2, 1, 3):
                q_x(0, 0, d).start()

    def split_f(i):
        slot = i % SLOTS
        load_f(i, slot).wait()
        for half in range(2):
            part = fst[slot, :, half * 1024:(half + 1) * 1024]
            high = part.astype(BF16)
            rows = pl.ds(pl.multiple_of(i * 128, 128), 128)
            fh[half, rows, :] = high
            fl[half, rows, :] = (part - high.astype(F32)).astype(BF16)

        @pl.when(i + SLOTS < 8)
        def _():
            load_f(i + SLOTS, slot).start()

    def forward(k):
        q_y(k).wait_recv()
        for d in (2, 1, 3):
            q_x(k, 4, d).start()
        if k + 1 < CHUNKS:
            for d in (2, 1, 3):
                q_x(k + 1, 0, d).start()

    forward(0)
    forward(1)
    lax.fori_loop(0, 4, lambda i, _: (split_f(i), 0)[1], 0)
    forward(2)
    lax.fori_loop(4, 8, lambda i, _: (split_f(i), 0)[1], 0)
    forward(3)
    load_e.start()

    def cross(k):
        return remote(pp.at[1 - c, 0:8 * SIZES[k]], cx.at[k % 2, 0:8 * SIZES[k]], cx_s.at[k], cx_r.at[k], sibling)

    def stage_a(k):
        own, m = SIZES[k], 8 * SIZES[k]
        if k + 4 < CHUNKS:
            forward(k + 4)
        for j in range(8):
            if j % 4:
                q_x(k, j // 4 * 4, j % 4).wait_recv()
            place = (((x + 4 - j % 4) % 4) * 2 + (yl + j // 4) % 2) * own
            rows = pl.ds(pl.multiple_of(place, 16), own)
            scale = qm[k][j, m:m + 16, :].astype(F32)[0:1]
            for b in range(8):
                value = decode(qm[k][j, b * own:(b + 1) * own, :], scale)
                high = value.astype(BF16)
                qh[rows, b * 128:(b + 1) * 128] = high
                ql[rows, b * 128:(b + 1) * 128] = (value - high.astype(F32)).astype(BF16)
        if k:
            cross(k - 1).wait_send()

        def product(half):
            @pl.loop(0, 2)
            def _(n):
                cols = pl.ds(pl.multiple_of(n * 512, 512), 512)
                total = jnp.dot(qh[0:m, :], fh[half, :, cols], preferred_element_type=F32)
                total += jnp.dot(qh[0:m, :], fl[half, :, cols], preferred_element_type=F32)
                total += jnp.dot(ql[0:m, :], fh[half, :, cols], preferred_element_type=F32)
                pp[half, 0:m, cols] = total

        product(1 - c)
        cross(k).start()
        product(c)

    def h_to(k):
        return remote(psend[k].at[pl.ds((1 - yh) * 4, 4)], pry[k], h_s.at[k], h_r.at[k], rpeer(4))

    def p_to(k, d):
        return remote(pair[k].at[(z + d) % 4], prx[k].at[d - 1], p_s.at[k, d], p_r.at[k, d], rpeer(d))

    def put_coded(m, tiles, ref, b):
        step = m // len(tiles)
        largest = functools.reduce(jnp.maximum, [fold_max(tile) for tile in tiles])
        scale, factor = scale_of(jnp.max(largest, axis=0, keepdims=True))
        for t, tile in enumerate(tiles):
            ref[b, t * step:(t + 1) * step, :] = code(tile, factor)
        ref[b, m:m + 16, :] = jnp.broadcast_to(scale, (16, 128)).astype(BF16)

    def stage_b(k):
        m = 8 * SIZES[k]
        step = m // 4
        cross(k).wait_recv()

        @pl.loop(0, 8)
        def _(b):
            cols = pl.ds(pl.multiple_of(b * 128, 128), 128)
            put_coded(m, [pp[c, t:t + step, cols] + cx[k % 2, t:t + step, cols] for t in range(0, m, step)], psend[k], b)

        h_to(k).start()

    def stage_r(k):
        m = 8 * SIZES[k]
        step = m // 4
        h_to(k).wait_recv()

        @pl.loop(0, 4)
        def _(b):
            mine_scale = psend[k][yh * 4 + b, m:m + 16, :].astype(F32)[0:1]
            scale = pry[k][b, m:m + 16, :].astype(F32)[0:1]
            put_coded(m, [decode(psend[k][yh * 4 + b, t:t + step, :], mine_scale) + decode(pry[k][b, t:t + step, :], scale)
                          for t in range(0, m, step)], pair[k], b)

        for d in (2, 1, 3):
            p_to(k, d).start()

    mine = c * 8 + chip

    def g_y(k):
        return remote(pf[k].at[mine], pf[k].at[mine], g_s.at[k, 4], g_r.at[k, 4], rpeer(4))

    def g_z(k, s, d):
        piece = c * 8 + chip_at(s)
        return remote(pf[k].at[piece], pf[k].at[piece], g_s.at[k, s + d], g_r.at[k, s + d], rpeer(d))

    def stage_c(k):
        m, step = 8 * SIZES[k], SIZES[k]
        for d in (1, 2, 3):
            p_to(k, d).wait_recv()
        scales = [pair[k][z, m:m + 16, :].astype(F32)[0:1]]
        scales += [prx[k][d, m:m + 16, :].astype(F32)[0:1] for d in range(3)]

        @pl.loop(0, 8)
        def _(t):
            rows = pl.ds(pl.multiple_of(t * step, 16), step)
            total = decode(pair[k][z, rows, :], scales[0])
            for d in range(3):
                total += decode(prx[k][d, rows, :], scales[d + 1])
            pf[k][mine, rows, :] = total.astype(BF16)

        g_y(k).start()
        for d in (1, 3, 2):
            g_z(k, 0, d).start()

    def stage_d(k):
        g_y(k).wait_recv()
        for d in (1, 3, 2):
            g_z(k, 4, d).start()

    def whole(k):
        return remote(pf[k].at[pl.ds(c * 8, 8)], pf[k].at[pl.ds(c * 8, 8)], k_s.at[k], k_r.at[k], sibling)

    def stage_k(k):
        for s in (0, 4):
            for d in (1, 3, 2):
                g_z(k, s, d).wait_recv()
        whole(k).start()

    def s_to(k, d, n=0):
        cols = slice(n * 512, (n + 1) * 512)
        if k in ACROSS:
            src, dst = ysend[k].at[(x + d) % 4], srx[k].at[d - 1, 0:SIZES[k]]
        else:
            src, dst = ss[k].at[(x + d) % 4, :, cols], srx[k].at[d - 1, :, cols]
        return remote(src, dst, s_s.at[k, n, d - 1], s_r.at[k, n, d - 1], xpeer(d))

    def y_to(k):
        own = SIZES[k]
        if k in ACROSS:
            src = ss[k].at[:, pl.ds(pl.multiple_of((1 - yl) * own, 16), own), :]
        else:
            src = ysend[k]
        return remote(src, yrx[k], y_s.at[k], y_r.at[k], ypeer)

    def stage_e(k):
        if k == 0:
            load_e.wait()
        whole(k).wait_recv()

        for n in range(3):
            rows = slice(n * 512, (n + 1) * 512)
            left = jnp.concatenate([pf[k][g] for g in range(16)], axis=1)
            total = lax.dot_general(left, e[rows, :], (((1,), (1,)), ((), ())), preferred_element_type=F32)
            ss[k][:, :, rows] = total.astype(BF16).reshape(4, 2 * SIZES[k], 512)
            if k not in ACROSS:
                for d in (2, 1, 3):
                    s_to(k, d, n).start()

        if k in ACROSS:
            y_to(k).start()

    def across(k):
        (group, first), own = PLACES[k], SIZES[k]
        y_to(k).wait_recv()

        def summed(b, t, cols):
            rows = pl.ds(pl.multiple_of(yl * own + t, 16), 16)
            return ss[k][b, rows, cols].astype(F32) + yrx[k][b, t:t + 16, cols].astype(F32)

        @pl.loop(0, 3)
        def _(n):
            cols = pl.ds(pl.multiple_of(n * 512, 512), 512)
            for t in range(0, own, 16):
                for b in range(4):
                    ysend[k][b, t:t + 16, cols] = summed(b, t, cols).astype(BF16)

        for d in (1, 3, 2):
            s_to(k, d).start()

        @pl.loop(0, 3)
        def _(n):
            cols = pl.ds(pl.multiple_of(n * 512, 512), 512)
            for t in range(0, own, 16):
                out[group, first + t:first + t + 16, cols] = summed(x, t, cols)

    def stage_g(k):
        if k in ACROSS:
            across(k)
            return
        (group, first), own = PLACES[k], SIZES[k]
        for n in range(3):
            for d in (1, 2, 3):
                s_to(k, d, n).wait_recv()

        def summed(part, rows, cols):
            rows = pl.ds(pl.multiple_of(part * own + rows, 16), 16)
            total = ss[k][x, rows, cols].astype(F32)
            for d in range(3):
                total += srx[k][d, rows, cols].astype(F32)
            return total

        @pl.loop(0, 3)
        def _(n):
            cols = pl.ds(pl.multiple_of(n * 512, 512), 512)
            for t in range(0, own, 16):
                ysend[k][t:t + 16, cols] = summed(1 - yl, t, cols).astype(BF16)

        y_to(k).start()

        @pl.loop(0, 3)
        def _(n):
            cols = pl.ds(pl.multiple_of(n * 512, 512), 512)
            for t in range(0, own, 16):
                out[group, first + t:first + t + 16, cols] = summed(yl, t, cols)

    def stage_h(k):
        (group, first), own = PLACES[k], SIZES[k]
        if k in ACROSS:
            for d in (1, 2, 3):
                s_to(k, d).wait_recv()
        else:
            y_to(k).wait_recv()

        @pl.loop(0, 3)
        def _(n):
            cols = pl.ds(pl.multiple_of(n * 512, 512), 512)
            if k in ACROSS:
                for t in range(0, own, 16):
                    rows = slice(first + t, first + t + 16)
                    out[group, rows, cols] += sum(srx[k][d, t:t + 16, cols].astype(F32) for d in range(3))
                return
            out[group, first:first + own, cols] += yrx[k][:, cols].astype(F32)

    stages = dict(A=stage_a, B=stage_b, R=stage_r, C=stage_c, D=stage_d, K=stage_k, E=stage_e, G=stage_g, H=stage_h)
    for turn in range(CHUNKS + max(late for _, late in PATTERN)):
        for name, late in PATTERN:
            if 0 <= turn - late < CHUNKS:
                stages[name](turn - late)

    for k in range(CHUNKS):
        q_y(k).wait_send()
        for s in (0, 4):
            for d in (1, 2, 3):
                q_x(k, s, d).wait_send()
                g_z(k, s, d).wait_send()
        h_to(k).wait_send()
        for d in (1, 2, 3):
            p_to(k, d).wait_send()
        g_y(k).wait_send()
        whole(k).wait_send()
        for n in range(1 if k in ACROSS else 3):
            for d in (1, 2, 3):
                s_to(k, d, n).wait_send()
        y_to(k).wait_send()
    cross(CHUNKS - 1).wait_send()


def body(queries, inverse_fisher, examples):
    dma = pltpu.SemaphoreType.DMA
    n = CHUNKS

    def each(shape):
        return [pltpu.VMEM(shape(o), BF16) for o in SIZES]

    return pl.pallas_call(
        kernel,
        out_shape=jax.ShapeDtypeStruct((2, 96, 1536), F32),
        in_specs=[pl.BlockSpec(memory_space=pltpu.VMEM), pl.BlockSpec(memory_space=pl.ANY),
                  pl.BlockSpec(memory_space=pl.ANY)],
        out_specs=pl.BlockSpec(memory_space=pltpu.VMEM),
        scratch_shapes=[
            pltpu.VMEM((BIG, 1024), BF16),
            pltpu.VMEM((BIG, 1024), BF16),
            pltpu.VMEM((SLOTS, 128, 2048), F32),
            pltpu.VMEM((2, 1024, 1024), BF16),
            pltpu.VMEM((2, 1024, 1024), BF16),
            pltpu.VMEM((1536, 2048), BF16),
            pltpu.VMEM((2, BIG, 1024), F32),
            pltpu.VMEM((2, BIG, 1024), F32),
            each(lambda o: (8, 8 * o + 16, 128)),
            each(lambda o: (8, 8 * o + 16, 128)),
            each(lambda o: (4, 8 * o + 16, 128)),
            each(lambda o: (4, 8 * o + 16, 128)),
            each(lambda o: (3, 8 * o + 16, 128)),
            each(lambda o: (16, 8 * o, 128)),
            each(lambda o: (4, 2 * o, 1536)),
            each(lambda o: (3, 2 * o, 1536)),
            [pltpu.VMEM((4, o, 1536) if k in ACROSS else (o, 1536), BF16) for k, o in enumerate(SIZES)],
            [pltpu.VMEM((4, o, 1536) if k in ACROSS else (o, 1536), BF16) for k, o in enumerate(SIZES)],
            dma((SLOTS,)), dma((1,)),
            dma((n, 8)), dma((n, 8)),
            dma((n,)), dma((n,)),
            dma((n,)), dma((n,)),
            dma((n, 4)), dma((n, 4)),
            dma((n, 8)), dma((n, 8)),
            dma((n,)), dma((n,)),
            dma((n, 3, 3)), dma((n, 3, 3)),
            dma((n,)), dma((n,)),
        ],
        compiler_params=pltpu.CompilerParams(
            collective_id=0, has_side_effects=True, vmem_limit_bytes=60 * 2**20),
        cost_estimate=pl.CostEstimate(flops=29_000_000_000, bytes_accessed=17_000_000, transcendentals=0),
        name="influence",
    )(queries, inverse_fisher, examples)


def solution(mesh):
    return jax.shard_map(
        body,
        mesh=mesh,
        in_specs=(P(None, "feat", "row"), P("row", "feat"), P("row", "feat")),
        out_specs=P(None, "feat", "row"),
        check_vma=False,
    )
```
